128 devices in a mesh: row: 32 (over x_hi, y, z), col: 4 (over x_lo, core).
Axes of the slice: x: 4 (x_hi: 2, x_lo: 2; x = x_hi * 2 + x_lo), y: 4, z: 4, core: 2. Of those that a mesh axis runs over, the one named last changes fastest.
Arguments:
- atom_feats: bfloat16 [20480, 128], P('row'), may hold values from -6 to 6
- atom_gain: float32 [128], replicated, may hold values from 0.1 to 1.9
- w_atom: bfloat16 [3, 128, 128], P(None, None, 'col'), may hold values from -0.5 to 0.5
- atom_pair: bfloat16 [16, 20480, 128], P(None, 'row'), may hold values from -80 to 80
- w_atom_bias: bfloat16 [16, 4], P(None, 'col'), may hold values from -2 to 2
- atom_counts: int32 [2560], P('row'), may hold values from 2 to 24, as said below
- token_single: bfloat16 [2560, 768], P('row'), may hold values from -3 to 3
- w_pool: bfloat16 [128, 768], replicated, may hold values from -2 to 2
- token_gain: float32 [2, 768], replicated, may hold values from 0.1 to 1.9
- w_attn: bfloat16 [2, 4, 768, 768], P(None, None, None, 'col'), may hold values from -0.21875 to 0.21875
- w_out: bfloat16 [2, 768, 768], P(None, 'col'), may hold values from -0.21875 to 0.21875
- pair: bfloat16 [2560, 2560, 128], P('row', 'col'), may hold values from -30 to 30
- w_bias: bfloat16 [2, 128, 16], replicated, may hold values from -1 to 1
Outputs:
- tokens_out: bfloat16 [2560, 768], P('row')
The draws below stay inside these ranges and needn't reach their ends.
Inputs may be any that keep to these rules, and one draw needn't show every extreme that they name: `atom_counts`: the first 640 tokens have 24 atoms each, every other token 2 or 3; counts sum to 20480.
All inputs are finite; a program needn't handle non-finite values.
Results may differ from the reference program's by a relative error of at most 0.02.
Values may be sent and summed in bfloat16 or wider, within the bound.
No kernel may reach another device: no remote copies, remote signals or barrier semaphores. Data moves between devices by JAX's collectives and lax.ppermute only.
A program may use at most 128 MiB of HBM per device.

```python
import math
import jax
import jax.numpy as jnp
from jax import lax

CT = 768
HEADS = 16
HD = 48
CZ = 128
CA = 128
AHEADS = 4
AHD = 32
CP = 16
QBLOCK = 32
WK = 128
REACH = 48
LAYERS = 2
MOSTA = 24
TQ = 80
N = 2560
ATOMS = 20480
N_ROW = 32


def sign_vector(key, length, salt_tag):
    coin_bits = jax.random.randint(jax.random.fold_in(key, salt_tag), (length,), 0, 2)
    return coin_bits.astype(jnp.float32) * 2.0 - 1.0


def draw_atom_counts(key, part):
    key = jax.random.fold_in(key, 5)
    tail_len = 3 * N // 4
    extras = jnp.array([1, 2, 2], jnp.int32)[jnp.arange(tail_len, dtype=jnp.int32) % 3]
    order = jax.random.permutation(key, tail_len)
    tail_counts = 1 + extras[order]
    head_counts = jnp.full((N // 4,), MOSTA, jnp.int32)
    return jnp.concatenate([head_counts, tail_counts]).astype(jnp.int32)


def draw_pair(key, part):
    key = jax.random.fold_in(key, 1)
    field_key = jax.random.fold_in(key, 0)
    field_draw = jnp.clip(jax.random.normal(field_key, (N, N, CZ), jnp.float32), -6.0, 6.0)
    return field_draw.astype(jnp.bfloat16)


def draw_w_bias(key, part):
    direction = sign_vector(key, CZ, 101)
    key = jax.random.fold_in(key, 2)
    noise_draw = jnp.clip(jax.random.normal(key, (LAYERS, CZ, HEADS), jnp.float32), -4.0, 4.0)
    return ((0.5 * noise_draw + direction[None, :, None]) / math.sqrt(CZ)).astype(jnp.bfloat16)


def draw_atom_pair(key, part):
    key = jax.random.fold_in(key, 3)
    field_key = jax.random.fold_in(key, 0)
    field_draw = jnp.clip(jax.random.normal(field_key, (CP, ATOMS, WK), jnp.float32), -6.0, 6.0)
    return field_draw.astype(jnp.bfloat16)


def draw_w_atom_bias(key, part):
    direction = sign_vector(key, CP, 202)
    key = jax.random.fold_in(key, 4)
    noise_draw = jnp.clip(jax.random.normal(key, (CP, AHEADS), jnp.float32), -4.0, 4.0)
    return ((0.5 * noise_draw + direction[:, None]) / math.sqrt(CP)).astype(jnp.bfloat16)


def block_levels(stream_key, shape, cuts, least, largest):
    gain = 1.0
    for axis_at, parts in cuts:
        heights = jax.random.uniform(jax.random.fold_in(jax.random.fold_in(stream_key, 6), axis_at), (parts,), jnp.float32, least / len(cuts), largest / len(cuts))
        gain = gain * jnp.repeat(jnp.exp(heights), shape[axis_at] // parts).reshape((-1,) + (1,) * (len(shape) - 1 - axis_at))
    return gain


def bell_draw(own_key, dims, width, most, pieces=(), kind=jnp.bfloat16):
    loudness = block_levels(own_key, dims, pieces, -0.22, 0.18) if pieces else 1.0
    result = jax.random.normal(own_key, dims, jnp.float32) * width * loudness
    return jnp.minimum(jnp.maximum(result, -most), most).astype(kind)


def setup_inputs(seed: int = 0) -> dict:
    arg_keys = jax.random.split(jax.random.key(seed), 14)
    return {
        "atom_feats": bell_draw(arg_keys[0], (ATOMS, CA), 1.0, 6.0, ((0, 32),)),
        "atom_gain": jnp.clip(1.0 + 0.18 * jax.random.normal(arg_keys[1], (CA,), jnp.float32), 0.1, 1.9),
        "w_atom": bell_draw(arg_keys[2], (3, CA, CA), CA ** -0.5, 0.5, ((2, 4),)),
        "atom_pair": draw_atom_pair(jax.random.fold_in(arg_keys[13], 71), 0),
        "w_atom_bias": draw_w_atom_bias(jax.random.fold_in(arg_keys[13], 71), 0),
        "atom_counts": draw_atom_counts(jax.random.fold_in(arg_keys[13], 71), 0),
        "token_single": bell_draw(arg_keys[6], (N, CT), 0.5, 3.0, ((0, 32),)),
        "w_pool": bell_draw(arg_keys[7], (CA, CT), (CA // 16) ** -0.5, 2.0),
        "token_gain": jnp.clip(1.0 + 0.18 * jax.random.normal(arg_keys[8], (LAYERS, CT), jnp.float32), 0.1, 1.9),
        "w_attn": bell_draw(arg_keys[9], (LAYERS, 4, CT, CT), CT ** -0.5, 0.21875, ((3, 4),)),
        "w_out": bell_draw(arg_keys[10], (LAYERS, CT, CT), CT ** -0.5, 0.21875, ((1, 4),)),
        "pair": draw_pair(jax.random.fold_in(arg_keys[13], 71), 0),
        "w_bias": draw_w_bias(jax.random.fold_in(arg_keys[13], 71), 0),
    }


epsilon = 1e-05

def layer_norm(values, gain_row):
    values = values.astype(jnp.float32)
    centred = values - lax.optimization_barrier(jnp.mean(values, axis=-1, keepdims=True))
    spread = lax.optimization_barrier(jnp.mean(centred * centred, axis=-1, keepdims=True))
    return centred * lax.rsqrt(spread + epsilon) * gain_row.astype(jnp.float32)

def softmax_rows(scores):
    row_max = lax.optimization_barrier(jnp.max(scores, axis=-1, keepdims=True))
    weights = jnp.exp(scores - row_max)
    return (weights / lax.optimization_barrier(jnp.sum(weights, axis=-1, keepdims=True))).astype(jnp.bfloat16)

def atom_windows(values):
    blocks = values.shape[0] // QBLOCK
    zero_rim = jnp.zeros((REACH, values.shape[1]), values.dtype)
    padded = jnp.concatenate([zero_rim, values, zero_rim], axis=0)
    atom_tiles = padded.reshape(blocks + WK // QBLOCK - 1, QBLOCK, values.shape[1])
    return jnp.concatenate([atom_tiles[offset:offset + blocks] for offset in range(WK // QBLOCK)], axis=1)

def reference(atom_feats, atom_gain, w_atom, atom_pair, w_atom_bias, atom_counts, token_single, w_pool, token_gain, w_attn, w_out, pair, w_bias):
    normed_atoms = layer_norm(atom_feats, atom_gain).astype(jnp.bfloat16)
    atom_q = jnp.dot(normed_atoms, w_atom[0], preferred_element_type=jnp.float32).astype(jnp.bfloat16)
    atom_k = jnp.dot(normed_atoms, w_atom[1], preferred_element_type=jnp.float32).astype(jnp.bfloat16)
    atom_v = jnp.dot(normed_atoms, w_atom[2], preferred_element_type=jnp.float32).astype(jnp.bfloat16)
    blocks = ATOMS // QBLOCK
    key_win = atom_windows(atom_k).reshape(blocks, WK, AHEADS, AHD).astype(jnp.float32)
    value_win = atom_windows(atom_v).reshape(blocks, WK, AHEADS, AHD).astype(jnp.float32)
    query_blk = atom_q.reshape(blocks, QBLOCK, AHEADS, AHD).astype(jnp.float32)
    atom_bias = jnp.einsum('cak,ch->hak', atom_pair.astype(jnp.float32), w_atom_bias.astype(jnp.float32))
    atom_bias = jnp.transpose(atom_bias.reshape(AHEADS, blocks, QBLOCK, WK), (1, 0, 2, 3))
    keys_at = QBLOCK * jnp.arange(blocks, dtype=jnp.int32)[:, None] - REACH + jnp.arange(WK, dtype=jnp.int32)[None, :]
    in_range = (keys_at >= 0) & (keys_at < ATOMS)
    atom_scores = jnp.einsum('bqhd,bkhd->bhqk', query_blk, key_win) / math.sqrt(AHD) + atom_bias
    atom_scores = jnp.where(in_range[:, None, None, :], atom_scores, -1e+30)
    atom_probs = softmax_rows(atom_scores)
    atom_out = jnp.einsum('bhqk,bkhd->bqhd', atom_probs.astype(jnp.float32), value_win)
    atom_out = atom_out.reshape(ATOMS, CA).astype(jnp.bfloat16)
    seg_ends = jnp.cumsum(atom_counts).astype(jnp.int32)
    seg_starts = (seg_ends - atom_counts).astype(jnp.int32)
    atom_index = jnp.arange(ATOMS, dtype=jnp.int32)
    member = ((atom_index[None, :] >= seg_starts[:, None]) & (atom_index[None, :] < seg_ends[:, None])).astype(jnp.bfloat16)
    token_sums = jnp.dot(member, atom_out, preferred_element_type=jnp.float32)
    pooled = (token_sums / atom_counts.astype(jnp.float32)[:, None]).astype(jnp.bfloat16)
    residual = token_single.astype(jnp.float32) + jnp.dot(pooled, w_pool, preferred_element_type=jnp.float32)
    for layer_idx in range(LAYERS):
        normed = layer_norm(residual, token_gain[layer_idx]).astype(jnp.bfloat16)
        projected = [jnp.dot(normed, w_attn[layer_idx, which], preferred_element_type=jnp.float32).astype(jnp.bfloat16) for which in range(4)]
        queries, key_rows, value_rows, gates = projected
        keys_all = key_rows.reshape(N, HEADS, HD).astype(jnp.float32)
        values_all = value_rows.reshape(N, HEADS, HD).astype(jnp.float32)
        bias_weight = w_bias[layer_idx].astype(jnp.float32)

        def attend(block_idx):
            pair_rows = lax.dynamic_slice_in_dim(pair, block_idx * TQ, TQ, 0).astype(jnp.float32)
            pair_bias = jnp.einsum('ijc,ch->hij', pair_rows, bias_weight).astype(jnp.bfloat16)
            query_rows = lax.dynamic_slice_in_dim(queries, block_idx * TQ, TQ, 0).reshape(TQ, HEADS, HD).astype(jnp.float32)
            scores = jnp.einsum('thd,nhd->htn', query_rows, keys_all) / math.sqrt(HD) + pair_bias.astype(jnp.float32)
            token_probs = softmax_rows(scores)
            mixture = jnp.einsum('htn,nhd->thd', token_probs.astype(jnp.float32), values_all).reshape(TQ, CT)
            gate_rows = lax.dynamic_slice_in_dim(gates, block_idx * TQ, TQ, 0).astype(jnp.float32)
            return (mixture * jax.nn.sigmoid(gate_rows)).astype(jnp.bfloat16)
        gated = lax.map(attend, jnp.arange(N_ROW, dtype=jnp.int32)).reshape(N, CT)
        residual = residual + jnp.dot(gated, w_out[layer_idx], preferred_element_type=jnp.float32)
    return residual.astype(jnp.bfloat16)
```

```python
import functools
import math

import jax
import jax.numpy as jnp
from jax import lax
from jax.experimental import pallas as pl
from jax.experimental.pallas import tpu as pltpu
from jax.sharding import Mesh
from jax.sharding import PartitionSpec as P

QBLOCK = 32
WK = 128
REACH = 48
EPSILON = 1e-05
NQ, NK, NC = 8, 4, 4
BF = jnp.bfloat16
F32 = jnp.float32
VMEM_LIMIT = 56 * 1024 * 1024
NT = (((1,), (1,)), ((), ()))
TN = (((0,), (0,)), ((), ()))


def dot(a, b, dims=(((1,), (0,)), ((), ()))):
    return lax.dot_general(a, b, dims, preferred_element_type=F32)


def layer_norm(values, gain_row):
    centred = values - jnp.mean(values, axis=-1, keepdims=True)
    spread = jnp.mean(centred * centred, axis=-1, keepdims=True)
    return centred * lax.rsqrt(spread + EPSILON) * gain_row


def call(kernel, out_shape, flops, moved, **kw):
    return pl.pallas_call(
        kernel,
        out_shape=out_shape,
        compiler_params=pltpu.CompilerParams(vmem_limit_bytes=VMEM_LIMIT),
        cost_estimate=pl.CostEstimate(flops=flops, bytes_accessed=moved, transcendentals=0),
        **kw,
    )


def shaped(shape, dtype):
    return jax.ShapeDtypeStruct(shape, dtype)


def pair_bias_kernel(pair_ref, w_ref, out_ref):
    rows = pair_ref.shape[0]
    w = w_ref[...]
    for i in range(rows):
        bias = dot(w, pair_ref[i], NT).astype(BF)
        out_ref[0, :, i, :] = bias[:16]
        out_ref[1, :, i, :] = bias[16:]


def pair_bias_call(pair, w_t):
    rows, cols, ch = pair.shape
    step = 16
    return pl.pallas_call(
        pair_bias_kernel,
        grid=(rows // step,),
        in_specs=[
            pl.BlockSpec((step, cols, ch), lambda i: (i, 0, 0)),
            pl.BlockSpec((32, ch), lambda i: (0, 0)),
        ],
        out_specs=pl.BlockSpec((2, 16, step, cols), lambda i: (0, 0, i, 0)),
        out_shape=shaped((2, 16, rows, cols), BF),
        compiler_params=pltpu.CompilerParams(vmem_limit_bytes=VMEM_LIMIT),
        cost_estimate=pl.CostEstimate(
            flops=2 * rows * cols * ch * 32, bytes_accessed=2 * rows * cols * (ch + 32), transcendentals=0
        ),
    )(pair, w_t)


def atom_kernel(first_ref, wab_ref, feats_ref, prev_ref, next_ref, gain_ref, w_ref, apair_ref, starts_ref, ends_ref, out_ref):
    rows = feats_ref.shape[0]
    first = first_ref[0]
    total = rows * NQ * NK
    x = jnp.concatenate([prev_ref[...], feats_ref[...], next_ref[...]], axis=0).astype(F32)
    normed = layer_norm(x, gain_ref[...]).astype(BF)
    q = dot(normed[REACH : REACH + rows], w_ref[0]).astype(BF)
    k = dot(normed, w_ref[1]).astype(BF)
    v = dot(normed, w_ref[2]).astype(BF)
    bias = apair_ref[0].astype(F32) * wab_ref[0]
    for c in range(1, apair_ref.shape[0]):
        bias += apair_ref[c].astype(F32) * wab_ref[c]
    scores = jnp.concatenate(
        [dot(q[at : at + QBLOCK], k[at : at + WK], NT) for at in range(0, rows, QBLOCK)], axis=0
    )
    scores = scores * (1.0 / math.sqrt(q.shape[1])) + bias
    at = lax.broadcasted_iota(jnp.int32, (rows, WK), 0) // QBLOCK * QBLOCK
    key_at = at + lax.broadcasted_iota(jnp.int32, (rows, WK), 1) + (first - REACH)
    scores = jnp.where((key_at >= 0) & (key_at < total), scores, -1e30)
    weights = jnp.exp(scores - jnp.max(scores, axis=-1, keepdims=True))
    probs = (weights / jnp.sum(weights, axis=-1, keepdims=True)).astype(BF)
    out = jnp.concatenate(
        [dot(probs[at : at + QBLOCK], v[at : at + WK]) for at in range(0, rows, QBLOCK)], axis=0
    )
    out_t = out.T.astype(BF)
    span = starts_ref.shape[2]
    index = lax.broadcasted_iota(jnp.int32, (rows, span), 0) + first
    for part in range(NQ):
        member = (index >= starts_ref[part]) & (index < ends_ref[part])
        member = jnp.where(member, 1.0, 0.0).astype(BF)
        out_ref[part] = dot(out_t, member).astype(BF)


def smem():
    return pl.BlockSpec(memory_space=pltpu.SMEM)


def vmem():
    return pl.BlockSpec(memory_space=pltpu.VMEM)


def project(residual, gain, w, kv_ref, qg_ref, width):
    normed = layer_norm(residual, gain).astype(BF)
    out = dot(normed, w).astype(BF)
    kv_ref[...] = out[:, : 2 * width]
    qg_ref[...] = out[:, 2 * width :]


def first_kernel(sums_ref, counts_ref, single_ref, w_pool_ref, gain_ref, w_ref, res_ref, kv_ref, qg_ref):
    sums = sums_ref[0].astype(F32)
    for k in range(1, NK):
        sums += sums_ref[k].astype(F32)
    pooled = (sums / counts_ref[...]).astype(BF)
    residual = single_ref[...].astype(F32) + dot(pooled, w_pool_ref[...], TN)
    res_ref[...] = residual
    project(residual, gain_ref[...], w_ref[...], kv_ref, qg_ref, kv_ref.shape[1] // 2)


def attend_kernel(qg_ref, kv_ref, bias_ref, out_ref):
    width = qg_ref.shape[1] // 2
    rows = bias_ref.shape[1]
    cols = bias_ref.shape[2]
    keys = kv_ref[:, :width]
    values = kv_ref[:, width:]
    for part in range(NK):
        q = qg_ref[part * rows : (part + 1) * rows, :width]
        scores = dot(q, keys, NT) * (1.0 / math.sqrt(width))
        bias = jnp.concatenate([bias_ref[part * NC + c] for c in range(NC)], axis=1)
        scores = scores + bias.astype(F32)
        weights = jnp.exp(scores - jnp.max(scores, axis=-1, keepdims=True))
        probs = (weights * (1.0 / jnp.sum(weights, axis=-1, keepdims=True))).astype(BF)
        mixture = dot(probs, values)
        gates = qg_ref[part * rows : (part + 1) * rows, width:].astype(F32)
        out_ref[part] = (mixture * jax.nn.sigmoid(gates)).T.astype(BF)


def middle_kernel(res_ref, gated_ref, w_out_ref, gain_ref, w_ref, out_ref, kv_ref, qg_ref):
    rows = gated_ref.shape[2]
    for part in range(NK):
        at = slice(part * rows, (part + 1) * rows)
        out_ref[at] = res_ref[at] + dot(gated_ref[part], w_out_ref[...], TN)
    project(out_ref[...], gain_ref[...], w_ref[...], kv_ref, qg_ref, kv_ref.shape[1] // 2)


def last_kernel(res_ref, gated_ref, w_out_ref, out_ref):
    out_ref[...] = (res_ref[...] + dot(gated_ref[...], w_out_ref[...], TN)).astype(BF)


def spread_all(x, axis, n):
    return lax.all_to_all(jnp.broadcast_to(x[None], (n,) + x.shape), axis, 0, 0, tiled=True)


def on_device(
    atom_feats, atom_gain, w_atom, atom_pair, w_atom_bias, atom_counts, token_single,
    w_pool, token_gain, w_attn, w_out, pair, w_bias,
):
    row_axes = ("q", "k")
    n_rows = NQ * NK
    q_at, k_at = lax.axis_index("q"), lax.axis_index("k")
    row_at = q_at * NK + k_at
    atom_rows, width_a = atom_feats.shape
    tq, ct = token_single.shape
    layers, ch, heads = w_bias.shape
    hd = ct // heads
    span = tq * NK

    prev = lax.ppermute(atom_feats[atom_rows - REACH :], row_axes, [(i, i + 1) for i in range(n_rows - 1)])
    nxt = lax.ppermute(atom_feats[:REACH], row_axes, [(i + 1, i) for i in range(n_rows - 1)])
    counts = jnp.pad(atom_counts, (0, 128 - tq))[None, None]
    counts = jnp.broadcast_to(counts, (n_rows, 8, 128))
    all_counts = lax.all_to_all(counts, row_axes, 0, 0, tiled=True)[:, 0, :tq].reshape(-1)
    singles = lax.all_gather(token_single, "k", axis=0, tiled=True)
    w_out_all = [
        lax.all_gather(w_out[l], "col", axis=0, tiled=False)
        .reshape(NC, NK, hd, ct).transpose(1, 0, 2, 3).reshape(ct, ct)
        for l in range(layers)
    ]
    w_own = lax.dynamic_slice_in_dim(w_attn, k_at * hd, hd, 3)
    w_cat = [
        jnp.concatenate([w_own[l, 1], w_own[l, 2], w_own[l, 0], w_own[l, 3]], axis=1) for l in range(layers)
    ]

    w_t = w_bias.reshape(layers, ch, NC, NK).transpose(0, 3, 2, 1).reshape(layers * heads, ch)
    local_bias = pair_bias_call(pair, w_t)
    bias = [lax.all_to_all(local_bias[l], ("k", "col"), 0, 0, tiled=True) for l in range(layers)]

    seg_ends = jnp.cumsum(all_counts)
    seg_starts = seg_ends - all_counts
    ends = seg_ends.reshape(NQ, 1, span)
    starts = seg_starts.reshape(NQ, 1, span)
    head_a = w_atom.shape[2]
    partial = call(
        atom_kernel,
        shaped((NQ, head_a, span), BF),
        2 * atom_rows * (3 * width_a * head_a + 2 * WK * head_a + head_a * NQ * span),
        2 * atom_pair.size,
        in_specs=[smem(), smem()] + [vmem()] * 8,
        out_specs=vmem(),
    )(
        (row_at * atom_rows).astype(jnp.int32)[None],
        w_atom_bias[:, 0].astype(F32),
        atom_feats, prev, nxt, atom_gain[None], w_atom, atom_pair, starts, ends,
    )
    sums = lax.all_to_all(partial, "q", 0, 0, tiled=True)
    sums = jnp.sum(sums.astype(F32), axis=0).astype(BF)
    sums = spread_all(sums, ("k", "col"), NK * NC).reshape(NK, width_a, span)
    own_counts = lax.dynamic_slice_in_dim(all_counts, q_at * span, span, 0).astype(F32)[None]

    proj_shapes = [shaped((span, ct), F32), shaped((span, 2 * hd), BF), shaped((span, 2 * hd), BF)]
    residual, kv, qg = call(first_kernel, proj_shapes, 2 * span * ct * 320, 2 * ct * 1000)(
        sums, own_counts, singles, w_pool, token_gain[0:1], w_cat[0]
    )
    for l in range(layers):
        kv = spread_all(kv, "q", NQ).reshape(NQ * span, 2 * hd)
        gated = call(
            attend_kernel, shaped((NK, hd, tq), BF), 4 * span * NQ * span * hd, 2 * bias[l].size
        )(qg, kv, bias[l])
        if l + 1 < layers:
            gated = spread_all(gated, ("k", "col"), NK * NC)
            gated = gated.transpose(1, 0, 2, 3).reshape(NK, ct, tq)
            residual, kv, qg = call(middle_kernel, proj_shapes, 2 * span * ct * 960, 2 * ct * 2000)(
                residual, gated, w_out_all[l], token_gain[l + 1 : l + 2], w_cat[l + 1]
            )
        else:
            gated = jnp.broadcast_to(gated[:, None], (NK, NC, hd, tq)).reshape(NK * NC, hd, tq)
            gated = lax.all_to_all(gated, ("k", "col"), 0, 0, tiled=True).reshape(ct, tq)
            own = lax.dynamic_slice_in_dim(residual, k_at * tq, tq, 0)
            return call(last_kernel, shaped((tq, ct), BF), 2 * tq * ct * ct, 2 * ct * ct)(
                own, gated, w_out_all[l]
            )


def solution(mesh):
    inner = Mesh(mesh.devices.reshape(NQ, NK, NC), ("q", "k", "col"))
    rows = ("q", "k")
    placed = (
        P(rows, None),
        P(),
        P(None, None, "col"),
        P(None, rows, None),
        P(None, "col"),
        P(rows),
        P(rows, None),
        P(),
        P(),
        P(None, None, None, "col"),
        P(None, "col", None),
        P(rows, "col", None),
        P(),
    )
    return jax.shard_map(
        on_device, mesh=inner, in_specs=placed, out_specs=P(rows, None), check_vma=False
    )
```

```python
import functools
import math

import jax
import jax.numpy as jnp
from jax import lax
from jax.experimental import pallas as pl
from jax.experimental.pallas import tpu as pltpu
from jax.sharding import PartitionSpec as P

QBLOCK = 32
WK = 128
REACH = 48
EPSILON = 1e-05
NC = 4
TOP, LANES = 16, 128
BF = jnp.bfloat16
F32 = jnp.float32
VMEM_LIMIT = 16 * 1024 * 1024
NT = (((1,), (1,)), ((), ()))
TN = (((0,), (0,)), ((), ()))


def dot(a, b, dims=(((1,), (0,)), ((), ()))):
    return lax.dot_general(a, b, dims, preferred_element_type=F32)


def layer_norm(values, gain_row):
    centred = values - jnp.mean(values, axis=-1, keepdims=True)
    spread = jnp.mean(centred * centred, axis=-1, keepdims=True)
    return centred * lax.rsqrt(spread + EPSILON) * gain_row


def call(kernel, out_shape, flops, moved, **kw):
    return pl.pallas_call(
        kernel,
        out_shape=out_shape,
        compiler_params=pltpu.CompilerParams(vmem_limit_bytes=VMEM_LIMIT),
        cost_estimate=pl.CostEstimate(flops=flops, bytes_accessed=moved, transcendentals=0),
        **kw,
    )


def shaped(shape, dtype):
    return jax.ShapeDtypeStruct(shape, dtype)


def pair_bias_kernel(col_ref, pair_ref, w_ref, *out_refs):
    total, own = w_ref.shape[0], out_refs[0].shape[0]
    to = lax.broadcasted_iota(jnp.int32, (total, total), 0)
    at = lax.broadcasted_iota(jnp.int32, (total, total), 1)
    heads = NC * own
    wanted = to // heads * heads + ((to % heads // own) ^ col_ref[0]) * own + to % own
    w = dot(jnp.where(at == wanted, 1.0, 0.0).astype(BF), w_ref[...]).astype(BF)
    for i in range(pair_ref.shape[0]):
        bias = dot(w, pair_ref[i], NT).astype(BF)
        for at, out_ref in enumerate(out_refs):
            out_ref[:, i, :] = bias[at * own : (at + 1) * own]


def pair_bias_call(col_at, pair, w_t, layers):
    rows, cols, ch = pair.shape
    own = w_t.shape[0] // (layers * NC)
    step = 16
    return pl.pallas_call(
        pair_bias_kernel,
        grid=(rows // step,),
        in_specs=[
            smem(),
            pl.BlockSpec((step, cols, ch), lambda i: (i, 0, 0)),
            pl.BlockSpec(w_t.shape, lambda i: (0, 0)),
        ],
        out_specs=[pl.BlockSpec((own, step, cols), lambda i: (0, i, 0))] * (layers * NC),
        out_shape=[shaped((own, rows, cols), BF)] * (layers * NC),
        compiler_params=pltpu.CompilerParams(vmem_limit_bytes=56 * 1024 * 1024),
        cost_estimate=pl.CostEstimate(
            flops=64 * rows * cols * ch, bytes_accessed=2 * rows * cols * (ch + 32), transcendentals=0
        ),
    )(col_at, pair, w_t)


def pack_kernel(row_ref, feats_ref, counts_ref, out_ref):
    rows = out_ref.shape[0]
    tq = counts_ref.shape[1]
    last = feats_ref.shape[0] - REACH
    counts = counts_ref[...].astype(F32)
    counts = jnp.concatenate([counts, jnp.zeros((1, LANES - tq), F32)], axis=1)
    top = jnp.where(lax.broadcasted_iota(jnp.int32, (TOP, LANES), 0) == 0, counts, 0.0).astype(BF)
    head = feats_ref[:REACH]
    for d in range(rows):
        out_ref[d, :TOP] = top
        out_ref[d, TOP:] = head

    @pl.when(row_ref[0] + 1 < rows)
    def _():
        out_ref[row_ref[0] + 1, TOP:] = feats_ref[last:]


def atom_kernel(row_ref, msg_ref, feats_ref, gain_ref, w_ref, wab_ref, apair_ref, out_ref, own_ref, counts_ref):
    rows = feats_ref.shape[0]
    n_rows = msg_ref.shape[0]
    tq = out_ref.shape[2]
    row = row_ref[0]
    first = row * rows
    total = rows * n_rows
    prev = msg_ref[jnp.maximum(row - 1, 0), TOP:]
    nxt = msg_ref[jnp.minimum(row + 1, n_rows - 1), TOP:]
    x = jnp.concatenate([prev, feats_ref[...], nxt], axis=0).astype(F32)
    normed = layer_norm(x, gain_ref[...]).astype(BF)
    q = dot(normed[REACH : REACH + rows], w_ref[0], NT).astype(BF)
    k = dot(normed, w_ref[1], NT).astype(BF)
    v = dot(normed, w_ref[2], NT).astype(BF)
    wab = wab_ref[...].astype(F32).T
    bias = apair_ref[0].astype(F32) * wab[0:1, 0:1]
    for c in range(1, apair_ref.shape[0]):
        bias += apair_ref[c].astype(F32) * wab[c : c + 1, 0:1]
    scores = jnp.concatenate(
        [dot(q[at : at + QBLOCK], k[at : at + WK], NT) for at in range(0, rows, QBLOCK)], axis=0
    )
    scores = scores * (1.0 / math.sqrt(q.shape[1])) + bias
    at = lax.broadcasted_iota(jnp.int32, (rows, WK), 0) // QBLOCK * QBLOCK
    key_at = at + lax.broadcasted_iota(jnp.int32, (rows, WK), 1) + (first - REACH)
    scores = jnp.where((key_at >= 0) & (key_at < total), scores, -1e30)
    weights = jnp.exp(scores - jnp.max(scores, axis=-1, keepdims=True))
    probs = (weights / jnp.sum(weights, axis=-1, keepdims=True)).astype(BF)
    out = jnp.concatenate(
        [dot(probs[at : at + QBLOCK], v[at : at + WK]) for at in range(0, rows, QBLOCK)], axis=0
    )
    out_t = out.T.astype(BF)

    counts = jnp.sum(msg_ref[:, :TOP].astype(F32), axis=1)
    small = counts.astype(BF)
    upto = lax.broadcasted_iota(jnp.int32, (LANES, LANES), 0) <= lax.broadcasted_iota(jnp.int32, (LANES, LANES), 1)
    inside = dot(small, jnp.where(upto, 1.0, 0.0).astype(BF))
    below = lax.broadcasted_iota(jnp.int32, (n_rows, n_rows), 1) < lax.broadcasted_iota(jnp.int32, (n_rows, n_rows), 0)
    before = jnp.sum(dot(jnp.where(below, 1.0, 0.0).astype(BF), small), axis=1, keepdims=True)
    ends = before + inside
    starts = ends - counts
    index = (lax.broadcasted_iota(jnp.int32, (rows, tq), 0) + first).astype(F32)
    for part in range(n_rows):
        start, end = starts[part : part + 1, :tq], ends[part : part + 1, :tq]
        member = jnp.where((index >= start) & (index < end), 1.0, 0.0).astype(BF)
        out_ref[part] = dot(out_t, member).astype(BF)
    counts_ref[...] = counts
    own_ref[...] = counts_ref[pl.ds(row, 1), :tq]


def sums_kernel(parts_ref, out_ref):
    sums = parts_ref[0].astype(F32)
    for part in range(1, parts_ref.shape[0]):
        sums += parts_ref[part].astype(F32)
    out_ref[...] = sums.astype(BF)


def smem():
    return pl.BlockSpec(memory_space=pltpu.SMEM)


def vmem():
    return pl.BlockSpec(memory_space=pltpu.VMEM)


def project(residual, gain, w_ref, kv_ref, qg_ref):
    width = w_ref.shape[2]
    normed = layer_norm(residual, gain).astype(BF)
    kv_ref[...] = dot(normed, w_ref[0, 1:3].reshape(2 * width, -1), NT).astype(BF)
    qg_ref[0] = dot(normed, w_ref[0, 0], NT).astype(BF)
    qg_ref[1] = dot(normed, w_ref[0, 3], NT).astype(BF)


def first_kernel(sums_ref, counts_ref, single_ref, w_pool_ref, gain_ref, w_ref, res_ref, kv_ref, qg_ref):
    pooled = (sums_ref[...].astype(F32) / counts_ref[...]).astype(BF)
    residual = single_ref[...].astype(F32) + dot(pooled, w_pool_ref[...], TN)
    res_ref[...] = residual
    project(residual, gain_ref[0:1], w_ref, kv_ref, qg_ref)


def spread_kernel(own_ref, far_ref, out_ref):
    for d in range(out_ref.shape[0]):
        out_ref[d, 0] = own_ref[...]
        out_ref[d, 1] = far_ref[...]


def attend_kernel(col_ref, half_ref, qg_ref, kv_ref, bias0_ref, bias1_ref, bias2_ref, bias3_ref, out_ref):
    own, rows, cols = bias0_ref.shape
    width = qg_ref.shape[2]
    hd = width // own
    wide = 2 * LANES
    skip = 2 * width - wide
    per = cols // rows
    lane = lax.broadcasted_iota(jnp.int32, (rows, wide), 1)
    q = jnp.concatenate([qg_ref[0], jnp.zeros((rows, wide - width), BF)], axis=1)
    q = jnp.concatenate(
        [jnp.where((lane >= h * hd) & (lane < (h + 1) * hd), q, jnp.zeros_like(q)) for h in range(own)], axis=0
    )
    scores, values = [], []
    for step, bias_ref in enumerate((bias0_ref, bias1_ref, bias2_ref, bias3_ref)):
        block = col_ref[0] ^ step
        at = block * per
        half = at // kv_ref.shape[0]
        kv = kv_ref[pl.ds(at - half * kv_ref.shape[0], per), half ^ half_ref[0]].reshape(cols, 2 * width)
        values.append(kv[:, skip:])
        part = dot(q, kv[:, :wide], NT) * (1.0 / math.sqrt(hd))
        scores.append(part + bias_ref[...].reshape(own * rows, cols).astype(F32))
    top = functools.reduce(jnp.maximum, [jnp.max(part, axis=-1, keepdims=True) for part in scores])
    weights = [jnp.exp(part - top) for part in scores]
    share = 1.0 / sum(jnp.sum(part, axis=-1, keepdims=True) for part in weights)
    mixture = sum(dot((part * share).astype(BF), v) for part, v in zip(weights, values))
    lane = lane - (wide - width)
    out = jnp.zeros((rows, wide), F32)
    for h in range(own):
        out = jnp.where((lane >= h * hd) & (lane < (h + 1) * hd), mixture[h * rows : (h + 1) * rows], out)
    out_ref[...] = (out[:, wide - width :] * jax.nn.sigmoid(qg_ref[1].astype(F32))).astype(BF)


def out_rows(col_ref, gated_ref, w_out_refs):
    return sum(dot(gated_ref[col_ref[0] ^ step], w_ref[0]) for step, w_ref in enumerate(w_out_refs))


def middle_kernel(col_ref, res_ref, gated_ref, w0_ref, w1_ref, w2_ref, w3_ref, gain_ref, w_ref, out_ref, kv_ref, qg_ref):
    residual = res_ref[...] + out_rows(col_ref, gated_ref, (w0_ref, w1_ref, w2_ref, w3_ref))
    out_ref[...] = residual
    project(residual, gain_ref[1:2], w_ref, kv_ref, qg_ref)


def last_kernel(col_ref, res_ref, gated_ref, w0_ref, w1_ref, w2_ref, w3_ref, out_ref):
    out_ref[...] = (res_ref[...] + out_rows(col_ref, gated_ref, (w0_ref, w1_ref, w2_ref, w3_ref))).astype(BF)


def exchange(x, axis):
    return lax.all_to_all(x, axis, 0, 0, tiled=True)


def from_step(x, step):
    return lax.ppermute(x, "col", [(i, i ^ step) for i in range(NC)])


def on_device(
    atom_feats, atom_gain, w_atom, atom_pair, w_atom_bias, atom_counts, token_single,
    w_pool, token_gain, w_attn, w_out, pair, w_bias,
):
    n_rows = lax.axis_size("row")
    half = n_rows // 2
    halves = [list(range(half)), list(range(half, n_rows))]
    row_at = lax.axis_index("row").astype(jnp.int32)[None]
    half_at = row_at // half
    col_at = lax.axis_index("col").astype(jnp.int32)[None]
    atom_rows, width_a = atom_feats.shape
    tq, ct = token_single.shape
    layers, ch, heads = w_bias.shape
    width = w_attn.shape[3]
    own = heads // NC

    msg = call(pack_kernel, shaped((n_rows, TOP + REACH, LANES), BF), 0, 1 << 19, in_specs=[smem(), vmem(), vmem()], out_specs=vmem())(
        row_at, atom_feats, atom_counts[None]
    )
    msg = exchange(msg, "row")

    w_t = w_bias.transpose(0, 2, 1).reshape(layers * heads, ch)
    local_bias = pair_bias_call(col_at, pair, w_t, layers)
    msg, *local_bias = lax.optimization_barrier((msg, *local_bias))

    def sent_bias(pieces):
        return [pieces[0]] + [from_step(pieces[step], step) for step in range(1, NC)]

    bias = sent_bias(local_bias[:NC])

    head_a = w_atom.shape[2]
    partial, own_counts = call(
        atom_kernel,
        [shaped((n_rows, head_a, tq), BF), shaped((1, tq), F32)],
        2 * atom_rows * (3 * width_a * head_a + 2 * WK * head_a + head_a * n_rows * tq),
        2 * atom_pair.size,
        in_specs=[smem()] + [vmem()] * 6,
        out_specs=[vmem()] * 2,
        scratch_shapes=[pltpu.VMEM((n_rows, LANES), F32)],
    )(row_at, msg, atom_feats, atom_gain[None], w_atom.transpose(0, 2, 1), w_atom_bias.T, atom_pair)
    sums = call(sums_kernel, shaped((head_a, tq), BF), 0, 1 << 18)(exchange(partial, "row"))
    sums = lax.all_gather(sums, "col", axis=0, tiled=True)
    sums, bias = lax.optimization_barrier((sums, bias))

    w_attn_t = w_attn.transpose(0, 1, 3, 2)
    proj = [shaped((tq, ct), F32), shaped((tq, 2 * width), BF), shaped((2, tq, width), BF)]

    def w_spec(l):
        return pl.BlockSpec((1, 4, width, ct), lambda i: (l, 0, 0, 0))

    def w_out_specs(l):
        return [pl.BlockSpec((1, width, ct), lambda i: (l, 0, 0))] * NC

    residual, kv, qg = call(
        first_kernel, proj, 2 * tq * ct * ct, 2 * ct * ct,
        grid=(1,), in_specs=[vmem()] * 5 + [w_spec(0)], out_specs=[vmem()] * 3,
    )(sums, own_counts, token_single, w_pool, token_gain, w_attn_t)
    for l in range(layers):
        far = lax.ppermute(kv, "row", [(i, (i + half) % n_rows) for i in range(n_rows)])
        if l:
            kv, far, bias = lax.optimization_barrier((kv, far, bias))
        kv = call(spread_kernel, shaped((half, 2) + kv.shape, BF), 0, 4 * half * kv.size, in_specs=[vmem()] * 2, out_specs=vmem())(
            kv, far
        )
        now = bias
        if not l:
            kv, w_out, *later = lax.optimization_barrier((kv, w_out, *local_bias[NC:]))
            bias = sent_bias(later)
            w_near, w_far = from_step(w_out, 1), from_step(w_out, 2)
        kv = lax.all_to_all(kv, "row", 0, 0, tiled=True, axis_index_groups=halves)
        if not l:
            kv, w_near, w_far = lax.optimization_barrier((kv, w_near, w_far))
            w_outs = [w_out, w_near, w_far, from_step(w_far, 1)]
        gated = call(
            attend_kernel, shaped((tq, width), BF), 4 * tq * n_rows * tq * width, 2 * heads * tq * n_rows * tq // NC,
            in_specs=[smem()] * 2 + [vmem()] * 6, out_specs=vmem(),
        )(col_at, half_at, qg, kv, *now)
        gated = lax.all_gather(gated, "col", axis=0, tiled=False)
        if l + 1 < layers:
            residual, kv, qg = call(
                middle_kernel, proj, 4 * tq * ct * ct, 4 * ct * ct,
                grid=(1,),
                in_specs=[smem(), vmem(), vmem()] + w_out_specs(l) + [vmem(), w_spec(l + 1)],
                out_specs=[vmem()] * 3,
            )(col_at, residual, gated, *w_outs, token_gain, w_attn_t)
    return call(
        last_kernel, shaped((tq, ct), BF), 2 * tq * ct * ct, 2 * ct * ct,
        grid=(1,), in_specs=[smem(), vmem(), vmem()] + w_out_specs(layers - 1), out_specs=vmem(),
    )(col_at, residual, gated, *w_outs)


def solution(mesh):
    placed = (
        P("row", None),
        P(),
        P(None, None, "col"),
        P(None, "row", None),
        P(None, "col"),
        P("row"),
        P("row", None),
        P(),
        P(),
        P(None, None, None, "col"),
        P(None, "col", None),
        P("row", "col", None),
        P(),
    )
    return jax.shard_map(
        on_device, mesh=mesh, in_specs=placed, out_specs=P("row", None), check_vma=False
    )
```

```python
import functools
import math

import jax
import jax.numpy as jnp
from jax import lax
from jax.experimental import pallas as pl
from jax.experimental.pallas import tpu as pltpu
from jax.sharding import PartitionSpec as P

QBLOCK = 32
WK = 128
REACH = 48
EPSILON = 1e-05
NC = 4
TOP, LANES = 16, 128
BF = jnp.bfloat16
F32 = jnp.float32
VMEM_LIMIT = 16 * 1024 * 1024
NT = (((1,), (1,)), ((), ()))
TN = (((0,), (0,)), ((), ()))


def dot(a, b, dims=(((1,), (0,)), ((), ()))):
    return lax.dot_general(a, b, dims, preferred_element_type=F32)


def layer_norm(values, gain_row):
    centred = values - jnp.mean(values, axis=-1, keepdims=True)
    spread = jnp.mean(centred * centred, axis=-1, keepdims=True)
    return centred * lax.rsqrt(spread + EPSILON) * gain_row


def call(kernel, out_shape, flops, moved, **kw):
    return pl.pallas_call(
        kernel,
        out_shape=out_shape,
        compiler_params=pltpu.CompilerParams(vmem_limit_bytes=VMEM_LIMIT),
        cost_estimate=pl.CostEstimate(flops=flops, bytes_accessed=moved, transcendentals=0),
        **kw,
    )


def shaped(shape, dtype):
    return jax.ShapeDtypeStruct(shape, dtype)


def pair_bias_kernel(col_ref, pair_ref, w_ref, *out_refs):
    total, own = w_ref.shape[0], out_refs[0].shape[0]
    to = lax.broadcasted_iota(jnp.int32, (total, total), 0)
    at = lax.broadcasted_iota(jnp.int32, (total, total), 1)
    heads = NC * own
    wanted = to // heads * heads + ((to % heads // own) ^ col_ref[0]) * own + to % own
    w = dot(jnp.where(at == wanted, 1.0, 0.0).astype(BF), w_ref[...]).astype(BF)
    for i in range(pair_ref.shape[0]):
        bias = dot(w, pair_ref[i], NT).astype(BF)
        for at, out_ref in enumerate(out_refs):
            out_ref[:, i, :] = bias[at * own : (at + 1) * own]


def pair_bias_call(col_at, pair, w_t, layers):
    rows, cols, ch = pair.shape
    own = w_t.shape[0] // (layers * NC)
    step = 16
    return pl.pallas_call(
        pair_bias_kernel,
        grid=(rows // step,),
        in_specs=[
            smem(),
            pl.BlockSpec((step, cols, ch), lambda i: (i, 0, 0)),
            pl.BlockSpec(w_t.shape, lambda i: (0, 0)),
        ],
        out_specs=[pl.BlockSpec((own, step, cols), lambda i: (0, i, 0))] * (layers * NC),
        out_shape=[shaped((own, rows, cols), BF)] * (layers * NC),
        compiler_params=pltpu.CompilerParams(vmem_limit_bytes=56 * 1024 * 1024),
        cost_estimate=pl.CostEstimate(
            flops=64 * rows * cols * ch, bytes_accessed=2 * rows * cols * (ch + 32), transcendentals=0
        ),
    )(col_at, pair, w_t)


def pack_kernel(row_ref, feats_ref, counts_ref, out_ref):
    rows = out_ref.shape[0]
    tq = counts_ref.shape[1]
    last = feats_ref.shape[0] - REACH
    counts = counts_ref[...].astype(F32)
    counts = jnp.concatenate([counts, jnp.zeros((1, LANES - tq), F32)], axis=1)
    top = jnp.where(lax.broadcasted_iota(jnp.int32, (TOP, LANES), 0) == 0, counts, 0.0).astype(BF)
    head = feats_ref[:REACH]
    for d in range(rows):
        out_ref[d, :TOP] = top
        out_ref[d, TOP:] = head

    @pl.when(row_ref[0] + 1 < rows)
    def _():
        out_ref[row_ref[0] + 1, TOP:] = feats_ref[last:]


def atom_kernel(row_ref, msg_ref, feats_ref, gain_ref, w_ref, wab_ref, apair_ref, out_ref, own_ref, counts_ref):
    rows = feats_ref.shape[0]
    n_rows = msg_ref.shape[0]
    tq = out_ref.shape[2]
    row = row_ref[0]
    first = row * rows
    total = rows * n_rows
    prev = msg_ref[jnp.maximum(row - 1, 0), TOP:]
    nxt = msg_ref[jnp.minimum(row + 1, n_rows - 1), TOP:]
    x = jnp.concatenate([prev, feats_ref[...], nxt], axis=0).astype(F32)
    normed = layer_norm(x, gain_ref[...]).astype(BF)
    q = dot(normed[REACH : REACH + rows], w_ref[0], NT).astype(BF)
    k = dot(normed, w_ref[1], NT).astype(BF)
    v = dot(normed, w_ref[2], NT).astype(BF)
    wab = wab_ref[...].astype(F32).T
    bias = apair_ref[0].astype(F32) * wab[0:1, 0:1]
    for c in range(1, apair_ref.shape[0]):
        bias += apair_ref[c].astype(F32) * wab[c : c + 1, 0:1]
    scores = jnp.concatenate(
        [dot(q[at : at + QBLOCK], k[at : at + WK], NT) for at in range(0, rows, QBLOCK)], axis=0
    )
    scores = scores * (1.0 / math.sqrt(q.shape[1])) + bias
    at = lax.broadcasted_iota(jnp.int32, (rows, WK), 0) // QBLOCK * QBLOCK
    key_at = at + lax.broadcasted_iota(jnp.int32, (rows, WK), 1) + (first - REACH)
    scores = jnp.where((key_at >= 0) & (key_at < total), scores, -1e30)
    weights = jnp.exp(scores - jnp.max(scores, axis=-1, keepdims=True))
    probs = (weights / jnp.sum(weights, axis=-1, keepdims=True)).astype(BF)
    out = jnp.concatenate(
        [dot(probs[at : at + QBLOCK], v[at : at + WK]) for at in range(0, rows, QBLOCK)], axis=0
    )
    out_t = out.T.astype(BF)

    counts = jnp.sum(msg_ref[:, :TOP].astype(F32), axis=1)
    small = counts.astype(BF)
    upto = lax.broadcasted_iota(jnp.int32, (LANES, LANES), 0) <= lax.broadcasted_iota(jnp.int32, (LANES, LANES), 1)
    inside = dot(small, jnp.where(upto, 1.0, 0.0).astype(BF))
    below = lax.broadcasted_iota(jnp.int32, (n_rows, n_rows), 1) < lax.broadcasted_iota(jnp.int32, (n_rows, n_rows), 0)
    before = jnp.sum(dot(jnp.where(below, 1.0, 0.0).astype(BF), small), axis=1, keepdims=True)
    ends = before + inside
    starts = ends - counts
    index = (lax.broadcasted_iota(jnp.int32, (rows, tq), 0) + first).astype(F32)
    for part in range(n_rows):
        start, end = starts[part : part + 1, :tq], ends[part : part + 1, :tq]
        member = jnp.where((index >= start) & (index < end), 1.0, 0.0).astype(BF)
        out_ref[part] = dot(out_t, member).astype(BF)
    counts_ref[...] = counts
    own_ref[...] = counts_ref[pl.ds(row, 1), :tq]


def sums_kernel(parts_ref, out_ref):
    sums = parts_ref[0].astype(F32)
    for part in range(1, parts_ref.shape[0]):
        sums += parts_ref[part].astype(F32)
    out_ref[...] = sums.astype(BF)


def smem():
    return pl.BlockSpec(memory_space=pltpu.SMEM)


def vmem():
    return pl.BlockSpec(memory_space=pltpu.VMEM)


def project(residual, gain, w_ref, kv_ref, qg_ref):
    width = w_ref.shape[2]
    normed = layer_norm(residual, gain).astype(BF)
    kv_ref[...] = dot(normed, w_ref[0, 1:3].reshape(2 * width, -1), NT).astype(BF)
    qg_ref[0] = dot(normed, w_ref[0, 0], NT).astype(BF)
    qg_ref[1] = dot(normed, w_ref[0, 3], NT).astype(BF)


def first_kernel(sums_ref, counts_ref, single_ref, w_pool_ref, gain_ref, w_ref, res_ref, kv_ref, qg_ref):
    pooled = (sums_ref[...].astype(F32) / counts_ref[...]).astype(BF)
    residual = single_ref[...].astype(F32) + dot(pooled, w_pool_ref[...], TN)
    res_ref[...] = residual
    project(residual, gain_ref[0:1], w_ref, kv_ref, qg_ref)


def spread_kernel(own_ref, far_ref, out_ref):
    for d in range(out_ref.shape[0]):
        out_ref[d, 0] = own_ref[...]
        out_ref[d, 1] = far_ref[...]


def attend_kernel(col_ref, half_ref, qg_ref, kv_ref, bias0_ref, bias1_ref, bias2_ref, bias3_ref, out_ref):
    own, rows, cols = bias0_ref.shape
    width = qg_ref.shape[2]
    hd = width // own
    wide = 2 * LANES
    skip = 2 * width - wide
    per = cols // rows
    lane = lax.broadcasted_iota(jnp.int32, (rows, wide), 1)
    q = jnp.concatenate([qg_ref[0], jnp.zeros((rows, wide - width), BF)], axis=1)
    q = jnp.concatenate(
        [jnp.where((lane >= h * hd) & (lane < (h + 1) * hd), q, jnp.zeros_like(q)) for h in range(own)], axis=0
    )
    scores, values = [], []
    for step, bias_ref in enumerate((bias0_ref, bias1_ref, bias2_ref, bias3_ref)):
        block = col_ref[0] ^ step
        at = block * per
        half = at // kv_ref.shape[0]
        kv = kv_ref[pl.ds(at - half * kv_ref.shape[0], per), half ^ half_ref[0]].reshape(cols, 2 * width)
        values.append(kv[:, skip:])
        part = dot(q, kv[:, :wide], NT) * (1.0 / math.sqrt(hd))
        scores.append(part + bias_ref[...].reshape(own * rows, cols).astype(F32))
    top = functools.reduce(jnp.maximum, [jnp.max(part, axis=-1, keepdims=True) for part in scores])
    weights = [jnp.exp(part - top) for part in scores]
    share = 1.0 / sum(jnp.sum(part, axis=-1, keepdims=True) for part in weights)
    mixture = sum(dot((part * share).astype(BF), v) for part, v in zip(weights, values))
    lane = lane - (wide - width)
    out = jnp.zeros((rows, wide), F32)
    for h in range(own):
        out = jnp.where((lane >= h * hd) & (lane < (h + 1) * hd), mixture[h * rows : (h + 1) * rows], out)
    out_ref[...] = (out[:, wide - width :] * jax.nn.sigmoid(qg_ref[1].astype(F32))).astype(BF)


def out_rows(col_ref, gated_ref, w_out_refs):
    return sum(dot(gated_ref[col_ref[0] ^ step], w_ref[...]) for step, w_ref in enumerate(w_out_refs))


def middle_kernel(col_ref, res_ref, gated_ref, w0_ref, w1_ref, w2_ref, w3_ref, gain_ref, w_ref, out_ref, kv_ref, qg_ref):
    residual = res_ref[...] + out_rows(col_ref, gated_ref, (w0_ref, w1_ref, w2_ref, w3_ref))
    out_ref[...] = residual
    project(residual, gain_ref[1:2], w_ref, kv_ref, qg_ref)


def last_kernel(col_ref, res_ref, gated_ref, w0_ref, w1_ref, w2_ref, w3_ref, out_ref):
    out_ref[...] = (res_ref[...] + out_rows(col_ref, gated_ref, (w0_ref, w1_ref, w2_ref, w3_ref))).astype(BF)


def exchange(x, axis):
    return lax.all_to_all(x, axis, 0, 0, tiled=True)


def from_step(x, step):
    return lax.ppermute(x, "col", [(i, i ^ step) for i in range(NC)])


def on_device(
    atom_feats, atom_gain, w_atom, atom_pair, w_atom_bias, atom_counts, token_single,
    w_pool, token_gain, w_attn, w_out, pair, w_bias,
):
    n_rows = lax.axis_size("row")
    half = n_rows // 2
    halves = [list(range(half)), list(range(half, n_rows))]
    row_at = lax.axis_index("row").astype(jnp.int32)[None]
    half_at = row_at // half
    col_at = lax.axis_index("col").astype(jnp.int32)[None]
    atom_rows, width_a = atom_feats.shape
    tq, ct = token_single.shape
    layers, ch, heads = w_bias.shape
    width = w_attn.shape[3]
    own = heads // NC

    msg = call(pack_kernel, shaped((n_rows, TOP + REACH, LANES), BF), 0, 1 << 19, in_specs=[smem(), vmem(), vmem()], out_specs=vmem())(
        row_at, atom_feats, atom_counts[None]
    )
    msg = exchange(msg, "row")

    w_t = w_bias.transpose(0, 2, 1).reshape(layers * heads, ch)
    local_bias = pair_bias_call(col_at, pair, w_t, layers)
    msg, *local_bias = lax.optimization_barrier((msg, *local_bias))

    head_a = w_atom.shape[2]
    partial, own_counts = call(
        atom_kernel,
        [shaped((n_rows, head_a, tq), BF), shaped((1, tq), F32)],
        2 * atom_rows * (3 * width_a * head_a + 2 * WK * head_a + head_a * n_rows * tq),
        2 * atom_pair.size,
        in_specs=[smem()] + [vmem()] * 6,
        out_specs=[vmem()] * 2,
        scratch_shapes=[pltpu.VMEM((n_rows, LANES), F32)],
    )(row_at, msg, atom_feats, atom_gain[None], w_atom.transpose(0, 2, 1), w_atom_bias.T, atom_pair)
    sums = call(sums_kernel, shaped((head_a, tq), BF), 0, 1 << 18)(exchange(partial, "row"))
    sums = lax.all_gather(sums, "col", axis=0, tiled=True)

    w_attn_t = w_attn.transpose(0, 1, 3, 2)
    proj = [shaped((tq, ct), F32), shaped((tq, 2 * width), BF), shaped((2, tq, width), BF)]

    def w_spec(l):
        return pl.BlockSpec((1, 4, width, ct), lambda i: (l, 0, 0, 0))

    residual, kv, qg = call(
        first_kernel, proj, 2 * tq * ct * ct, 2 * ct * ct,
        grid=(1,), in_specs=[vmem()] * 5 + [w_spec(0)], out_specs=[vmem()] * 3,
    )(sums, own_counts, token_single, w_pool, token_gain, w_attn_t)
    for l in range(layers):
        far = lax.ppermute(kv, "row", [(i, (i + half) % n_rows) for i in range(n_rows)])
        pieces = local_bias[l * NC : (l + 1) * NC]
        kv, far, w_own, *pieces = lax.optimization_barrier((kv, far, w_out[l], *pieces))
        kv = call(spread_kernel, shaped((half, 2) + kv.shape, BF), 0, 4 * half * kv.size, in_specs=[vmem()] * 2, out_specs=vmem())(
            kv, far
        )
        w_far = from_step(w_own, 2)
        now = [pieces[0]] + [from_step(pieces[step], step) for step in range(1, NC)]
        moved = [from_step(w_own, 1), w_far, from_step(w_far, 1)]
        kv = lax.all_to_all(kv, "row", 0, 0, tiled=True, axis_index_groups=halves)
        kv, *moved = lax.optimization_barrier((kv, *moved))
        w_outs = [w_own] + moved
        gated = call(
            attend_kernel, shaped((tq, width), BF), 4 * tq * n_rows * tq * width, 2 * heads * tq * n_rows * tq // NC,
            in_specs=[smem()] * 2 + [vmem()] * 6, out_specs=vmem(),
        )(col_at, half_at, qg, kv, *now)
        gated = lax.all_gather(gated, "col", axis=0, tiled=False)
        if l + 1 < layers:
            residual, kv, qg = call(
                middle_kernel, proj, 4 * tq * ct * ct, 4 * ct * ct,
                grid=(1,),
                in_specs=[smem()] + [vmem()] * 7 + [w_spec(l + 1)],
                out_specs=[vmem()] * 3,
            )(col_at, residual, gated, *w_outs, token_gain, w_attn_t)
    return call(
        last_kernel, shaped((tq, ct), BF), 2 * tq * ct * ct, 2 * ct * ct,
        in_specs=[smem()] + [vmem()] * 6, out_specs=vmem(),
    )(col_at, residual, gated, *w_outs)


def solution(mesh):
    placed = (
        P("row", None),
        P(),
        P(None, None, "col"),
        P(None, "row", None),
        P(None, "col"),
        P("row"),
        P("row", None),
        P(),
        P(),
        P(None, None, None, "col"),
        P(None, "col", None),
        P("row", "col", None),
        P(),
    )
    return jax.shard_map(
        on_device, mesh=mesh, in_specs=placed, out_specs=P("row", None), check_vma=False
    )
```

```python
import functools
import math

import jax
import jax.numpy as jnp
from jax import lax
from jax.experimental import pallas as pl
from jax.experimental.pallas import tpu as pltpu
from jax.sharding import PartitionSpec as P

QBLOCK = 32
WK = 128
REACH = 48
EPSILON = 1e-05
NC = 4
TOP, LANES = 16, 128
BF = jnp.bfloat16
F32 = jnp.float32
VMEM_LIMIT = 16 * 1024 * 1024
WHOLE_VMEM = 56 * 1024 * 1024
NT = (((1,), (1,)), ((), ()))
TN = (((0,), (0,)), ((), ()))


def dot(a, b, dims=(((1,), (0,)), ((), ()))):
    return lax.dot_general(a, b, dims, preferred_element_type=F32)


def layer_norm(values, gain_row):
    centred = values - jnp.mean(values, axis=-1, keepdims=True)
    spread = jnp.mean(centred * centred, axis=-1, keepdims=True)
    return centred * lax.rsqrt(spread + EPSILON) * gain_row


def call(kernel, out_shape, flops, moved, limit=VMEM_LIMIT, **kw):
    return pl.pallas_call(
        kernel,
        out_shape=out_shape,
        compiler_params=pltpu.CompilerParams(vmem_limit_bytes=limit),
        cost_estimate=pl.CostEstimate(flops=flops, bytes_accessed=moved, transcendentals=0),
        **kw,
    )


def shaped(shape, dtype):
    return jax.ShapeDtypeStruct(shape, dtype)


def pair_bias_kernel(col_ref, pair_ref, w_ref, *out_refs):
    total, own = w_ref.shape[0], out_refs[0].shape[0]
    to = lax.broadcasted_iota(jnp.int32, (total, total), 0)
    at = lax.broadcasted_iota(jnp.int32, (total, total), 1)
    heads = NC * own
    wanted = to // heads * heads + ((to % heads // own) ^ col_ref[0]) * own + to % own
    w = dot(jnp.where(at == wanted, 1.0, 0.0).astype(BF), w_ref[...]).astype(BF)
    for i in range(pair_ref.shape[0]):
        bias = dot(w, pair_ref[i], NT).astype(BF)
        for at, out_ref in enumerate(out_refs):
            out_ref[:, i, :] = bias[at * own : (at + 1) * own]


def pair_bias_call(col_at, pair, w_t, layers):
    rows, cols, ch = pair.shape
    own = w_t.shape[0] // (layers * NC)
    step = 16
    return pl.pallas_call(
        pair_bias_kernel,
        grid=(rows // step,),
        in_specs=[
            smem(),
            pl.BlockSpec((step, cols, ch), lambda i: (i, 0, 0)),
            pl.BlockSpec(w_t.shape, lambda i: (0, 0)),
        ],
        out_specs=[pl.BlockSpec((own, step, cols), lambda i: (0, i, 0))] * (layers * NC),
        out_shape=[shaped((own, rows, cols), BF)] * (layers * NC),
        compiler_params=pltpu.CompilerParams(vmem_limit_bytes=WHOLE_VMEM),
        cost_estimate=pl.CostEstimate(
            flops=64 * rows * cols * ch, bytes_accessed=2 * rows * cols * (ch + 32), transcendentals=0
        ),
    )(col_at, pair, w_t)


def pack_kernel(row_ref, feats_ref, gain_ref, w_ref, counts_ref, out_ref):
    rows = out_ref.shape[0]
    tq = counts_ref.shape[1]
    half = LANES // 2
    last = feats_ref.shape[0] - REACH
    edges = jnp.concatenate([feats_ref[:REACH], feats_ref[last:]], axis=0).astype(F32)
    normed = layer_norm(edges, gain_ref[...]).astype(BF)
    kv = jnp.concatenate([dot(normed, w_ref[1], NT), dot(normed, w_ref[2], NT)], axis=1)
    counts = counts_ref[...].astype(F32)
    rest = jnp.concatenate([counts[:, half:], jnp.zeros((1, LANES - tq), F32)], axis=1)
    at = lax.broadcasted_iota(jnp.int32, (TOP, half), 0)
    counts = jnp.where(at == 0, counts[:, :half], jnp.where(at == 1, rest, 0.0))

    def message(kv):
        right = jnp.concatenate([kv[2 * TOP :], counts], axis=0)
        return jnp.concatenate([kv[: 2 * TOP], right], axis=1).astype(BF)

    head = message(kv[:REACH])
    for d in range(rows):
        out_ref[d] = head

    @pl.when(row_ref[0] + 1 < rows)
    def _():
        out_ref[row_ref[0] + 1] = message(kv[REACH:])


def atom_kernel(row_ref, msg_ref, feats_ref, gain_ref, w_ref, wab_ref, apair_ref, out_ref, own_ref, counts_ref):
    rows = feats_ref.shape[0]
    n_rows = msg_ref.shape[0]
    tq = out_ref.shape[2]
    half = LANES // 2
    row = row_ref[0]
    first = row * rows
    total = rows * n_rows
    prev = msg_ref[jnp.maximum(row - 1, 0)].astype(F32)
    nxt = msg_ref[jnp.minimum(row + 1, n_rows - 1)].astype(F32)
    normed = layer_norm(feats_ref[...].astype(F32), gain_ref[...]).astype(BF)
    q = dot(normed, w_ref[0], NT).astype(BF)
    own = jnp.concatenate([dot(normed, w_ref[1], NT), dot(normed, w_ref[2], NT)], axis=1)
    kv = jnp.concatenate(
        [prev[:, :half], prev[:TOP, half:], own, nxt[:, :half], nxt[:TOP, half:]], axis=0
    ).astype(BF)
    k, v = kv[:, : half // 2], kv[:, half // 2 :]
    wab = wab_ref[...].astype(F32).T
    bias = apair_ref[0].astype(F32) * wab[0:1, 0:1]
    for c in range(1, apair_ref.shape[0]):
        bias += apair_ref[c].astype(F32) * wab[c : c + 1, 0:1]
    scores = jnp.concatenate(
        [dot(q[at : at + QBLOCK], k[at : at + WK], NT) for at in range(0, rows, QBLOCK)], axis=0
    )
    scores = scores * (1.0 / math.sqrt(q.shape[1])) + bias
    at = lax.broadcasted_iota(jnp.int32, (rows, WK), 0) // QBLOCK * QBLOCK
    key_at = at + lax.broadcasted_iota(jnp.int32, (rows, WK), 1) + (first - REACH)
    scores = jnp.where((key_at >= 0) & (key_at < total), scores, -1e30)
    weights = jnp.exp(scores - jnp.max(scores, axis=-1, keepdims=True))
    probs = (weights / jnp.sum(weights, axis=-1, keepdims=True)).astype(BF)
    out = jnp.concatenate(
        [dot(probs[at : at + QBLOCK], v[at : at + WK]) for at in range(0, rows, QBLOCK)], axis=0
    )
    out_t = out.T.astype(BF)

    held = msg_ref[:, TOP:].astype(F32)
    at = lax.broadcasted_iota(jnp.int32, held.shape, 1)
    counts = jnp.concatenate(
        [jnp.sum(jnp.where(at == i, held, 0.0), axis=1)[:, half:] for i in range(2)], axis=1
    )
    small = counts.astype(BF)
    upto = lax.broadcasted_iota(jnp.int32, (LANES, LANES), 0) <= lax.broadcasted_iota(jnp.int32, (LANES, LANES), 1)
    inside = dot(small, jnp.where(upto, 1.0, 0.0).astype(BF))
    below = lax.broadcasted_iota(jnp.int32, (n_rows, n_rows), 1) < lax.broadcasted_iota(jnp.int32, (n_rows, n_rows), 0)
    before = jnp.sum(dot(jnp.where(below, 1.0, 0.0).astype(BF), small), axis=1, keepdims=True)
    ends = before + inside
    starts = ends - counts
    index = (lax.broadcasted_iota(jnp.int32, (rows, tq), 0) + first).astype(F32)
    for part in range(n_rows):
        start, end = starts[part : part + 1, :tq], ends[part : part + 1, :tq]
        member = jnp.where((index >= start) & (index < end), 1.0, 0.0).astype(BF)
        out_ref[part] = dot(out_t, member).astype(BF)
    counts_ref[...] = counts
    own_ref[...] = counts_ref[pl.ds(row, 1), :tq]


def sums_kernel(parts_ref, out_ref):
    sums = parts_ref[0].astype(F32)
    for part in range(1, parts_ref.shape[0]):
        sums += parts_ref[part].astype(F32)
    out_ref[...] = sums.astype(BF)


def smem():
    return pl.BlockSpec(memory_space=pltpu.SMEM)


def vmem():
    return pl.BlockSpec(memory_space=pltpu.VMEM)


def project(residual, gain, w_ref, kv_ref, qg_ref):
    width = w_ref.shape[2]
    normed = layer_norm(residual, gain).astype(BF)
    kv_ref[...] = dot(normed, w_ref[0, 1:3].reshape(2 * width, -1), NT).astype(BF)
    qg_ref[0] = dot(normed, w_ref[0, 0], NT).astype(BF)
    qg_ref[1] = dot(normed, w_ref[0, 3], NT).astype(BF)


def first_kernel(sums_ref, counts_ref, single_ref, w_pool_ref, gain_ref, w_ref, res_ref, kv_ref, qg_ref):
    pooled = (sums_ref[...].astype(F32) / counts_ref[...]).astype(BF)
    residual = single_ref[...].astype(F32) + dot(pooled, w_pool_ref[...], TN)
    res_ref[...] = residual
    project(residual, gain_ref[0:1], w_ref, kv_ref, qg_ref)


def spread_kernel(own_ref, far_ref, out_ref):
    for d in range(out_ref.shape[0]):
        out_ref[d, 0] = own_ref[...]
        out_ref[d, 1] = far_ref[...]


def attend_kernel(col_ref, half_ref, qg_ref, kv_ref, bias0_ref, bias1_ref, bias2_ref, bias3_ref, out_ref):
    own, rows, cols = bias0_ref.shape
    width = qg_ref.shape[2]
    hd = width // own
    wide = 2 * LANES
    skip = 2 * width - wide
    per = cols // rows
    lane = lax.broadcasted_iota(jnp.int32, (rows, wide), 1)
    q = jnp.concatenate([qg_ref[0], jnp.zeros((rows, wide - width), BF)], axis=1)
    q = jnp.concatenate(
        [jnp.where((lane >= h * hd) & (lane < (h + 1) * hd), q, jnp.zeros_like(q)) for h in range(own)], axis=0
    )
    scores, values = [], []
    for step, bias_ref in enumerate((bias0_ref, bias1_ref, bias2_ref, bias3_ref)):
        block = col_ref[0] ^ step
        at = block * per
        half = at // kv_ref.shape[0]
        kv = kv_ref[pl.ds(at - half * kv_ref.shape[0], per), half ^ half_ref[0]].reshape(cols, 2 * width)
        values.append(kv[:, skip:])
        part = dot(q, kv[:, :wide], NT) * (1.0 / math.sqrt(hd))
        scores.append(part + bias_ref[...].reshape(own * rows, cols).astype(F32))
    top = functools.reduce(jnp.maximum, [jnp.max(part, axis=-1, keepdims=True) for part in scores])
    weights = [jnp.exp(part - top) for part in scores]
    share = 1.0 / sum(jnp.sum(part, axis=-1, keepdims=True) for part in weights)
    mixture = sum(dot((part * share).astype(BF), v) for part, v in zip(weights, values))
    lane = lane - (wide - width)
    out = jnp.zeros((rows, wide), F32)
    for h in range(own):
        out = jnp.where((lane >= h * hd) & (lane < (h + 1) * hd), mixture[h * rows : (h + 1) * rows], out)
    out_ref[...] = (out[:, wide - width :] * jax.nn.sigmoid(qg_ref[1].astype(F32))).astype(BF)


def out_rows(col_ref, gated_ref, w_out_refs):
    return sum(dot(gated_ref[col_ref[0] ^ step], w_ref[...]) for step, w_ref in enumerate(w_out_refs))


def middle_kernel(col_ref, res_ref, gated_ref, w0_ref, w1_ref, w2_ref, w3_ref, gain_ref, w_ref, out_ref, kv_ref, qg_ref):
    residual = res_ref[...] + out_rows(col_ref, gated_ref, (w0_ref, w1_ref, w2_ref, w3_ref))
    out_ref[...] = residual
    project(residual, gain_ref[1:2], w_ref, kv_ref, qg_ref)


def last_kernel(col_ref, res_ref, gated_ref, w0_ref, w1_ref, w2_ref, w3_ref, out_ref):
    out_ref[...] = (res_ref[...] + out_rows(col_ref, gated_ref, (w0_ref, w1_ref, w2_ref, w3_ref))).astype(BF)


def exchange(x, axis):
    return lax.all_to_all(x, axis, 0, 0, tiled=True)


def from_step(x, step):
    return lax.ppermute(x, "col", [(i, i ^ step) for i in range(NC)])


def on_device(
    atom_feats, atom_gain, w_atom, atom_pair, w_atom_bias, atom_counts, token_single,
    w_pool, token_gain, w_attn, w_out, pair, w_bias,
):
    n_rows = lax.axis_size("row")
    half = n_rows // 2
    halves = [list(range(half)), list(range(half, n_rows))]
    row_at = lax.axis_index("row").astype(jnp.int32)[None]
    half_at = row_at // half
    col_at = lax.axis_index("col").astype(jnp.int32)[None]
    atom_rows, width_a = atom_feats.shape
    tq, ct = token_single.shape
    layers, ch, heads = w_bias.shape
    width = w_attn.shape[3]
    own = heads // NC

    w_atom_t = w_atom.transpose(0, 2, 1)
    msg = call(
        pack_kernel, shaped((n_rows, 2 * TOP, LANES), BF), 0, 1 << 18, limit=WHOLE_VMEM,
        in_specs=[smem()] + [vmem()] * 4, out_specs=vmem(),
    )(row_at, atom_feats, atom_gain[None], w_atom_t, atom_counts[None])
    msg = exchange(msg, "row")

    head_a = w_atom.shape[2]
    partial, own_counts = call(
        atom_kernel,
        [shaped((n_rows, head_a, tq), BF), shaped((1, tq), F32)],
        2 * atom_rows * (3 * width_a * head_a + 2 * WK * head_a + head_a * n_rows * tq),
        2 * atom_pair.size,
        limit=WHOLE_VMEM,
        in_specs=[smem()] + [vmem()] * 6,
        out_specs=[vmem()] * 2,
        scratch_shapes=[pltpu.VMEM((n_rows, LANES), F32)],
    )(row_at, msg, atom_feats, atom_gain[None], w_atom_t, w_atom_bias.T, atom_pair)

    w_t = w_bias.transpose(0, 2, 1).reshape(layers * heads, ch)
    partial, w_t = lax.optimization_barrier((partial, w_t))
    parts = exchange(partial, "row")
    local_bias = pair_bias_call(col_at, pair, w_t, layers)
    parts, *local_bias = lax.optimization_barrier((parts, *local_bias))
    sums = call(sums_kernel, shaped((head_a, tq), BF), 0, 1 << 18)(parts)
    sums = lax.all_gather(sums, "col", axis=0, tiled=True)

    w_attn_t = w_attn.transpose(0, 1, 3, 2)
    proj = [shaped((tq, ct), F32), shaped((tq, 2 * width), BF), shaped((2, tq, width), BF)]

    def w_spec(l):
        return pl.BlockSpec((1, 4, width, ct), lambda i: (l, 0, 0, 0))

    residual, kv, qg = call(
        first_kernel, proj, 2 * tq * ct * ct, 2 * ct * ct,
        grid=(1,), in_specs=[vmem()] * 5 + [w_spec(0)], out_specs=[vmem()] * 3,
    )(sums, own_counts, token_single, w_pool, token_gain, w_attn_t)
    for l in range(layers):
        far = lax.ppermute(kv, "row", [(i, (i + half) % n_rows) for i in range(n_rows)])
        pieces = local_bias[l * NC : (l + 1) * NC]
        kv, far, w_own, *pieces = lax.optimization_barrier((kv, far, w_out[l], *pieces))
        kv = call(spread_kernel, shaped((half, 2) + kv.shape, BF), 0, 4 * half * kv.size, in_specs=[vmem()] * 2, out_specs=vmem())(
            kv, far
        )
        w_far = from_step(w_own, 2)
        now = [pieces[0]] + [from_step(pieces[step], step) for step in range(1, NC)]
        moved = [from_step(w_own, 1), w_far, from_step(w_far, 1)]
        kv = lax.all_to_all(kv, "row", 0, 0, tiled=True, axis_index_groups=halves)
        kv, *moved = lax.optimization_barrier((kv, *moved))
        w_outs = [w_own] + moved
        gated = call(
            attend_kernel, shaped((tq, width), BF), 4 * tq * n_rows * tq * width, 2 * heads * tq * n_rows * tq // NC,
            in_specs=[smem()] * 2 + [vmem()] * 6, out_specs=vmem(),
        )(col_at, half_at, qg, kv, *now)
        gated = lax.all_gather(gated, "col", axis=0, tiled=False)
        if l + 1 < layers:
            residual, kv, qg = call(
                middle_kernel, proj, 4 * tq * ct * ct, 4 * ct * ct,
                grid=(1,),
                in_specs=[smem()] + [vmem()] * 7 + [w_spec(l + 1)],
                out_specs=[vmem()] * 3,
            )(col_at, residual, gated, *w_outs, token_gain, w_attn_t)
    return call(
        last_kernel, shaped((tq, ct), BF), 2 * tq * ct * ct, 2 * ct * ct,
        in_specs=[smem()] + [vmem()] * 6, out_specs=vmem(),
    )(col_at, residual, gated, *w_outs)


def solution(mesh):
    placed = (
        P("row", None),
        P(),
        P(None, None, "col"),
        P(None, "row", None),
        P(None, "col"),
        P("row"),
        P("row", None),
        P(),
        P(),
        P(None, None, None, "col"),
        P(None, "col", None),
        P("row", "col", None),
        P(),
    )
    return jax.shard_map(
        on_device, mesh=mesh, in_specs=placed, out_specs=P("row", None), check_vma=False
    )
```

```python
import functools
import math

import jax
import jax.numpy as jnp
from jax import lax
from jax.experimental import pallas as pl
from jax.experimental.pallas import tpu as pltpu
from jax.sharding import PartitionSpec as P

QBLOCK = 32
WK = 128
REACH = 48
EPSILON = 1e-05
NC = 4
TOP, LANES = 16, 128
BF = jnp.bfloat16
F32 = jnp.float32
VMEM_LIMIT = 16 * 1024 * 1024
WHOLE_VMEM = 56 * 1024 * 1024
NT = (((1,), (1,)), ((), ()))
TN = (((0,), (0,)), ((), ()))


def dot(a, b, dims=(((1,), (0,)), ((), ()))):
    return lax.dot_general(a, b, dims, preferred_element_type=F32)


def layer_norm(values, gain_row):
    centred = values - jnp.mean(values, axis=-1, keepdims=True)
    spread = jnp.mean(centred * centred, axis=-1, keepdims=True)
    return centred * lax.rsqrt(spread + EPSILON) * gain_row


def call(kernel, out_shape, flops, moved, limit=VMEM_LIMIT, **kw):
    return pl.pallas_call(
        kernel,
        out_shape=out_shape,
        compiler_params=pltpu.CompilerParams(vmem_limit_bytes=limit),
        cost_estimate=pl.CostEstimate(flops=flops, bytes_accessed=moved, transcendentals=0),
        **kw,
    )


def shaped(shape, dtype):
    return jax.ShapeDtypeStruct(shape, dtype)


def pair_bias_kernel(col_ref, pair_ref, w_ref, *out_refs):
    total, own = w_ref.shape[0], out_refs[0].shape[0]
    to = lax.broadcasted_iota(jnp.int32, (total, total), 0)
    at = lax.broadcasted_iota(jnp.int32, (total, total), 1)
    heads = NC * own
    wanted = to // heads * heads + ((to % heads // own) ^ col_ref[0]) * own + to % own
    w = dot(jnp.where(at == wanted, 1.0, 0.0).astype(BF), w_ref[...]).astype(BF)
    for i in range(pair_ref.shape[0]):
        bias = dot(w, pair_ref[i], NT).astype(BF)
        for at, out_ref in enumerate(out_refs):
            out_ref[:, i, :] = bias[at * own : (at + 1) * own]


def pair_bias_call(col_at, pair, w_t, layers):
    rows, cols, ch = pair.shape
    own = w_t.shape[0] // (layers * NC)
    step = 16
    return pl.pallas_call(
        pair_bias_kernel,
        grid=(rows // step,),
        in_specs=[
            smem(),
            pl.BlockSpec((step, cols, ch), lambda i: (i, 0, 0)),
            pl.BlockSpec(w_t.shape, lambda i: (0, 0)),
        ],
        out_specs=[pl.BlockSpec((own, step, cols), lambda i: (0, i, 0))] * (layers * NC),
        out_shape=[shaped((own, rows, cols), BF)] * (layers * NC),
        compiler_params=pltpu.CompilerParams(vmem_limit_bytes=WHOLE_VMEM),
        cost_estimate=pl.CostEstimate(
            flops=64 * rows * cols * ch, bytes_accessed=2 * rows * cols * (ch + 32), transcendentals=0
        ),
    )(col_at, pair, w_t)


def pack_kernel(row_ref, feats_ref, gain_ref, w_ref, counts_ref, out_ref):
    rows = out_ref.shape[0]
    tq = counts_ref.shape[1]
    half = LANES // 2
    last = feats_ref.shape[0] - REACH
    edges = jnp.concatenate([feats_ref[:REACH], feats_ref[last:]], axis=0).astype(F32)
    normed = layer_norm(edges, gain_ref[...]).astype(BF)
    kv = jnp.concatenate([dot(normed, w_ref[1], NT), dot(normed, w_ref[2], NT)], axis=1)
    counts = counts_ref[...].astype(F32)
    rest = jnp.concatenate([counts[:, half:], jnp.zeros((1, LANES - tq), F32)], axis=1)
    at = lax.broadcasted_iota(jnp.int32, (TOP, half), 0)
    counts = jnp.where(at == 0, counts[:, :half], jnp.where(at == 1, rest, 0.0))

    def message(kv):
        right = jnp.concatenate([kv[2 * TOP :], counts], axis=0)
        return jnp.concatenate([kv[: 2 * TOP], right], axis=1).astype(BF)

    head = message(kv[:REACH])
    for d in range(rows):
        out_ref[d] = head

    @pl.when(row_ref[0] + 1 < rows)
    def _():
        out_ref[row_ref[0] + 1] = message(kv[REACH:])


def atom_own_kernel(feats_ref, gain_ref, w_ref, wab_ref, apair_ref, q_ref, kv_ref, bias_ref):
    normed = layer_norm(feats_ref[...].astype(F32), gain_ref[...]).astype(BF)
    q_ref[...] = dot(normed, w_ref[0], NT).astype(BF)
    kv_ref[...] = jnp.concatenate([dot(normed, w_ref[1], NT), dot(normed, w_ref[2], NT)], axis=1).astype(BF)
    wab = wab_ref[...].astype(F32).T
    bias = apair_ref[0].astype(F32) * wab[0:1, 0:1]
    for c in range(1, apair_ref.shape[0]):
        bias += apair_ref[c].astype(F32) * wab[c : c + 1, 0:1]
    bias_ref[...] = bias


def atom_kernel(row_ref, msg_ref, q_ref, kv_ref, bias_ref, out_ref, own_ref, counts_ref):
    rows = q_ref.shape[0]
    n_rows = msg_ref.shape[0]
    tq = out_ref.shape[2]
    half = LANES // 2
    row = row_ref[0]
    first = row * rows
    total = rows * n_rows
    prev = msg_ref[jnp.maximum(row - 1, 0)].astype(F32)
    nxt = msg_ref[jnp.minimum(row + 1, n_rows - 1)].astype(F32)
    q, bias = q_ref[...], bias_ref[...]
    kv = jnp.concatenate(
        [prev[:, :half], prev[:TOP, half:], kv_ref[...].astype(F32), nxt[:, :half], nxt[:TOP, half:]], axis=0
    ).astype(BF)
    k, v = kv[:, : half // 2], kv[:, half // 2 :]
    scores = jnp.concatenate(
        [dot(q[at : at + QBLOCK], k[at : at + WK], NT) for at in range(0, rows, QBLOCK)], axis=0
    )
    scores = scores * (1.0 / math.sqrt(q.shape[1])) + bias
    at = lax.broadcasted_iota(jnp.int32, (rows, WK), 0) // QBLOCK * QBLOCK
    key_at = at + lax.broadcasted_iota(jnp.int32, (rows, WK), 1) + (first - REACH)
    scores = jnp.where((key_at >= 0) & (key_at < total), scores, -1e30)
    weights = jnp.exp(scores - jnp.max(scores, axis=-1, keepdims=True))
    probs = (weights / jnp.sum(weights, axis=-1, keepdims=True)).astype(BF)
    out = jnp.concatenate(
        [dot(probs[at : at + QBLOCK], v[at : at + WK]) for at in range(0, rows, QBLOCK)], axis=0
    )
    out_t = out.T.astype(BF)

    held = msg_ref[:, TOP:].astype(F32)
    at = lax.broadcasted_iota(jnp.int32, held.shape, 1)
    counts = jnp.concatenate(
        [jnp.sum(jnp.where(at == i, held, 0.0), axis=1)[:, half:] for i in range(2)], axis=1
    )
    small = counts.astype(BF)
    upto = lax.broadcasted_iota(jnp.int32, (LANES, LANES), 0) <= lax.broadcasted_iota(jnp.int32, (LANES, LANES), 1)
    inside = dot(small, jnp.where(upto, 1.0, 0.0).astype(BF))
    below = lax.broadcasted_iota(jnp.int32, (n_rows, n_rows), 1) < lax.broadcasted_iota(jnp.int32, (n_rows, n_rows), 0)
    before = jnp.sum(dot(jnp.where(below, 1.0, 0.0).astype(BF), small), axis=1, keepdims=True)
    ends = before + inside
    starts = ends - counts
    index = (lax.broadcasted_iota(jnp.int32, (rows, tq), 0) + first).astype(F32)
    for part in range(n_rows):
        start, end = starts[part : part + 1, :tq], ends[part : part + 1, :tq]
        member = jnp.where((index >= start) & (index < end), 1.0, 0.0).astype(BF)
        out_ref[part] = dot(out_t, member).astype(BF)
    counts_ref[...] = counts
    own_ref[...] = counts_ref[pl.ds(row, 1), :tq]


def sums_kernel(parts_ref, out_ref):
    sums = parts_ref[0].astype(F32)
    for part in range(1, parts_ref.shape[0]):
        sums += parts_ref[part].astype(F32)
    out_ref[...] = sums.astype(BF)


def smem():
    return pl.BlockSpec(memory_space=pltpu.SMEM)


def vmem():
    return pl.BlockSpec(memory_space=pltpu.VMEM)


def project(residual, gain, w_ref, kv_ref, qg_ref):
    width = w_ref.shape[2]
    normed = layer_norm(residual, gain).astype(BF)
    kv_ref[...] = dot(normed, w_ref[0, 1:3].reshape(2 * width, -1), NT).astype(BF)
    qg_ref[0] = dot(normed, w_ref[0, 0], NT).astype(BF)
    qg_ref[1] = dot(normed, w_ref[0, 3], NT).astype(BF)


def first_kernel(sums_ref, counts_ref, single_ref, w_pool_ref, gain_ref, w_ref, res_ref, kv_ref, qg_ref):
    pooled = (sums_ref[...].astype(F32) / counts_ref[...]).astype(BF)
    residual = single_ref[...].astype(F32) + dot(pooled, w_pool_ref[...], TN)
    res_ref[...] = residual
    project(residual, gain_ref[0:1], w_ref, kv_ref, qg_ref)


def spread_kernel(own_ref, far_ref, out_ref):
    for d in range(out_ref.shape[0]):
        out_ref[d, 0] = own_ref[...]
        out_ref[d, 1] = far_ref[...]


def attend_kernel(col_ref, half_ref, qg_ref, kv_ref, bias0_ref, bias1_ref, bias2_ref, bias3_ref, out_ref):
    own, rows, cols = bias0_ref.shape
    width = qg_ref.shape[2]
    hd = width // own
    wide = 2 * LANES
    skip = 2 * width - wide
    per = cols // rows
    lane = lax.broadcasted_iota(jnp.int32, (rows, wide), 1)
    q = jnp.concatenate([qg_ref[0], jnp.zeros((rows, wide - width), BF)], axis=1)
    q = jnp.concatenate(
        [jnp.where((lane >= h * hd) & (lane < (h + 1) * hd), q, jnp.zeros_like(q)) for h in range(own)], axis=0
    )
    scores, values = [], []
    for step, bias_ref in enumerate((bias0_ref, bias1_ref, bias2_ref, bias3_ref)):
        block = col_ref[0] ^ step
        at = block * per
        half = at // kv_ref.shape[0]
        kv = kv_ref[pl.ds(at - half * kv_ref.shape[0], per), half ^ half_ref[0]].reshape(cols, 2 * width)
        values.append(kv[:, skip:])
        part = dot(q, kv[:, :wide], NT) * (1.0 / math.sqrt(hd))
        scores.append(part + bias_ref[...].reshape(own * rows, cols).astype(F32))
    top = functools.reduce(jnp.maximum, [jnp.max(part, axis=-1, keepdims=True) for part in scores])
    weights = [jnp.exp(part - top) for part in scores]
    share = 1.0 / sum(jnp.sum(part, axis=-1, keepdims=True) for part in weights)
    mixture = sum(dot((part * share).astype(BF), v) for part, v in zip(weights, values))
    lane = lane - (wide - width)
    out = jnp.zeros((rows, wide), F32)
    for h in range(own):
        out = jnp.where((lane >= h * hd) & (lane < (h + 1) * hd), mixture[h * rows : (h + 1) * rows], out)
    out_ref[...] = (out[:, wide - width :] * jax.nn.sigmoid(qg_ref[1].astype(F32))).astype(BF)


def out_rows(col_ref, gated_ref, w_out_refs):
    return sum(dot(gated_ref[col_ref[0] ^ step], w_ref[...]) for step, w_ref in enumerate(w_out_refs))


def middle_kernel(col_ref, res_ref, gated_ref, w0_ref, w1_ref, w2_ref, w3_ref, gain_ref, w_ref, out_ref, kv_ref, qg_ref):
    residual = res_ref[...] + out_rows(col_ref, gated_ref, (w0_ref, w1_ref, w2_ref, w3_ref))
    out_ref[...] = residual
    project(residual, gain_ref[1:2], w_ref, kv_ref, qg_ref)


def last_kernel(col_ref, res_ref, gated_ref, w0_ref, w1_ref, w2_ref, w3_ref, out_ref):
    out_ref[...] = (res_ref[...] + out_rows(col_ref, gated_ref, (w0_ref, w1_ref, w2_ref, w3_ref))).astype(BF)


def exchange(x, axis):
    return lax.all_to_all(x, axis, 0, 0, tiled=True)


def from_step(x, step):
    return lax.ppermute(x, "col", [(i, i ^ step) for i in range(NC)])


def on_device(
    atom_feats, atom_gain, w_atom, atom_pair, w_atom_bias, atom_counts, token_single,
    w_pool, token_gain, w_attn, w_out, pair, w_bias,
):
    n_rows = lax.axis_size("row")
    half = n_rows // 2
    halves = [list(range(half)), list(range(half, n_rows))]
    row_at = lax.axis_index("row").astype(jnp.int32)[None]
    half_at = row_at // half
    col_at = lax.axis_index("col").astype(jnp.int32)[None]
    atom_rows, width_a = atom_feats.shape
    tq, ct = token_single.shape
    layers, ch, heads = w_bias.shape
    width = w_attn.shape[3]
    own = heads // NC

    w_atom_t = w_atom.transpose(0, 2, 1)
    msg = call(
        pack_kernel, shaped((n_rows, 2 * TOP, LANES), BF), 0, 1 << 18, limit=WHOLE_VMEM,
        in_specs=[smem()] + [vmem()] * 4, out_specs=vmem(),
    )(row_at, atom_feats, atom_gain[None], w_atom_t, atom_counts[None])
    msg = exchange(msg, "row")

    head_a = w_atom.shape[2]
    own_atoms = call(
        atom_own_kernel,
        [shaped((atom_rows, head_a), BF), shaped((atom_rows, 2 * head_a), BF), shaped((atom_rows, WK), F32)],
        2 * atom_rows * 3 * width_a * head_a, 2 * atom_pair.size, limit=WHOLE_VMEM,
        in_specs=[vmem()] * 5, out_specs=[vmem()] * 3,
    )(atom_feats, atom_gain[None], w_atom_t, w_atom_bias.T, atom_pair)
    partial, own_counts = call(
        atom_kernel,
        [shaped((n_rows, head_a, tq), BF), shaped((1, tq), F32)],
        2 * atom_rows * (2 * WK * head_a + head_a * n_rows * tq), 1 << 20, limit=WHOLE_VMEM,
        in_specs=[smem()] + [vmem()] * 4,
        out_specs=[vmem()] * 2,
        scratch_shapes=[pltpu.VMEM((n_rows, LANES), F32)],
    )(row_at, msg, *own_atoms)

    w_t = w_bias.transpose(0, 2, 1).reshape(layers * heads, ch)
    partial, w_t = lax.optimization_barrier((partial, w_t))
    parts = exchange(partial, "row")
    local_bias = pair_bias_call(col_at, pair, w_t, layers)
    parts, *local_bias = lax.optimization_barrier((parts, *local_bias))
    sums = call(sums_kernel, shaped((head_a, tq), BF), 0, 1 << 18)(parts)
    sums = lax.all_gather(sums, "col", axis=0, tiled=True)

    w_attn_t = w_attn.transpose(0, 1, 3, 2)
    proj = [shaped((tq, ct), F32), shaped((tq, 2 * width), BF), shaped((2, tq, width), BF)]

    def w_spec(l):
        return pl.BlockSpec((1, 4, width, ct), lambda i: (l, 0, 0, 0))

    residual, kv, qg = call(
        first_kernel, proj, 2 * tq * ct * ct, 2 * ct * ct,
        grid=(1,), in_specs=[vmem()] * 5 + [w_spec(0)], out_specs=[vmem()] * 3,
    )(sums, own_counts, token_single, w_pool, token_gain, w_attn_t)
    for l in range(layers):
        far = lax.ppermute(kv, "row", [(i, (i + half) % n_rows) for i in range(n_rows)])
        pieces = local_bias[l * NC : (l + 1) * NC]
        kv, far, w_own, *pieces = lax.optimization_barrier((kv, far, w_out[l], *pieces))
        kv = call(spread_kernel, shaped((half, 2) + kv.shape, BF), 0, 4 * half * kv.size, in_specs=[vmem()] * 2, out_specs=vmem())(
            kv, far
        )
        w_far = from_step(w_own, 2)
        now = [pieces[0]] + [from_step(pieces[step], step) for step in range(1, NC)]
        moved = [from_step(w_own, 1), w_far, from_step(w_far, 1)]
        kv = lax.all_to_all(kv, "row", 0, 0, tiled=True, axis_index_groups=halves)
        kv, *moved = lax.optimization_barrier((kv, *moved))
        w_outs = [w_own] + moved
        gated = call(
            attend_kernel, shaped((tq, width), BF), 4 * tq * n_rows * tq * width, 2 * heads * tq * n_rows * tq // NC,
            in_specs=[smem()] * 2 + [vmem()] * 6, out_specs=vmem(),
        )(col_at, half_at, qg, kv, *now)
        gated = lax.all_gather(gated, "col", axis=0, tiled=False)
        if l + 1 < layers:
            residual, kv, qg = call(
                middle_kernel, proj, 4 * tq * ct * ct, 4 * ct * ct,
                grid=(1,),
                in_specs=[smem()] + [vmem()] * 7 + [w_spec(l + 1)],
                out_specs=[vmem()] * 3,
            )(col_at, residual, gated, *w_outs, token_gain, w_attn_t)
    return call(
        last_kernel, shaped((tq, ct), BF), 2 * tq * ct * ct, 2 * ct * ct,
        in_specs=[smem()] + [vmem()] * 6, out_specs=vmem(),
    )(col_at, residual, gated, *w_outs)


def solution(mesh):
    placed = (
        P("row", None),
        P(),
        P(None, None, "col"),
        P(None, "row", None),
        P(None, "col"),
        P("row"),
        P("row", None),
        P(),
        P(),
        P(None, None, None, "col"),
        P(None, "col", None),
        P("row", "col", None),
        P(),
    )
    return jax.shard_map(
        on_device, mesh=mesh, in_specs=placed, out_specs=P("row", None), check_vma=False
    )
```
